256 devices in a mesh: wide: 32 (over y, x, core), rep: 8 (over z).
Axes of the slice: x: 4, y: 4, z: 8, core: 2. Of those that a mesh axis runs over, the one named last changes fastest.
Arguments:
- queries: bfloat16 [2048, 128, 576], P(('rep', 'wide')), parts along dimension 0, may hold values from -16 to 16
- latent_cache: bfloat16 [2048, 384, 576], P(('rep', 'wide')), parts along dimension 0, may hold values from -4 to 4
- lengths: int32 [2048], P(('rep', 'wide')), parts along dimension 0, may hold values from 1 to 384, as said below
- occupied: int32 [2048], P(('rep', 'wide')), parts along dimension 0, may hold values 0 or 1
- residual: bfloat16 [2048, 3584], P(('rep', 'wide')), parts along dimension 0, may hold values from -4 to 4
- w_uv: bfloat16 [128, 512, 128], P('wide'), may hold values from -0.25 to 0.25
- w_out: bfloat16 [16384, 3584], P('wide'), may hold values from -0.046875 to 0.046875
- norm_gain: bfloat16 [3584], replicated, may hold values from 0.5 to 1.5
- w_gate: bfloat16 [3584, 9216], P(None, 'wide'), may hold values from -0.09375 to 0.09375
- w_up: bfloat16 [3584, 9216], P(None, 'wide'), may hold values from -0.09375 to 0.09375
- w_down: bfloat16 [9216, 3584], P('wide'), may hold values from -0.0625 to 0.0625
Outputs:
- layer_out: bfloat16 [2048, 3584], P(('rep', 'wide')), parts along dimension 0
The draws below stay inside these ranges and needn't reach their ends.
There are 8 independent parts, one for each index of `rep`. The reference program is written for one: setup_inputs(seed, part) draws one part's arguments, and reference() takes and returns one part's arrays. A program takes and returns all parts, laid end to end along the dimension named above; an argument that names none is the same for every part. Nothing has to cross between parts.
Inputs may be any that keep to these rules, and one draw needn't show every extreme that they name: `lengths`: some slot has length 384 in every draw.
All inputs are finite; a program needn't handle non-finite values. No bound on the sum of `occupied` on one device may be relied on, other than what follows from the above.
Results may differ from the reference program's by a relative error of at most 0.009.
Values may be sent and summed in bfloat16 or wider, within the bound.
A program may use at most 64 MiB of HBM per device.

```python
import jax
import jax.numpy as jnp
from jax import lax

D = 3584
HEADS = 128
LAT = 512
ROPE = 64
VHEAD = 128
FF = 9216
SLOT = 8
LMAX = 384
SLOTS = 256


def cache_values(key):
    base = jax.random.fold_in(key, 11)
    return jnp.clip(jax.random.normal(base, (SLOTS, LMAX, LAT + ROPE), jnp.float32), -4.0, 4.0)


def draw_latent_cache(key, part):
    return cache_values(key).astype(jnp.bfloat16)


def draw_queries(key, part):
    key = jax.random.fold_in(key, 2)
    drawn = jnp.clip(jax.random.normal(jax.random.fold_in(key, 1), (SLOTS, HEADS, LAT + ROPE), jnp.float32), -4.0, 4.0)
    return drawn.astype(jnp.bfloat16)


def draw_lengths(key, part):
    key = jax.random.fold_in(key, 7)
    groups = SLOTS // SLOT
    caps = jax.random.randint(jax.random.fold_in(key, 1), (groups, 1), LMAX // 8, LMAX + 1)
    raw = jax.random.randint(jax.random.fold_in(key, 2), (groups, SLOT), 0, 1 << 20)
    counts = (1 + raw % caps).reshape(SLOTS)
    longest = jax.random.randint(jax.random.fold_in(key, 3), (), 0, SLOTS)
    counts = counts.at[longest].set(LMAX)
    return counts.astype(jnp.int32)


def set_ends(values, key, low, high):
    spot = [jax.random.randint(jax.random.fold_in(key, axis), (), 0, length) for axis, length in enumerate(values.shape)]
    widest = values.shape.index(max(values.shape))
    beside = spot[:widest] + [(spot[widest] + 1) % values.shape[widest]] + spot[widest + 1:]
    return values.at[tuple(spot)].set(low).at[tuple(beside)].set(high)


def level_of(stream_key, shape, pieces, smallest, top_value):
    level, own = 1.0, jax.random.fold_in(stream_key, 6)
    for axis_at, parts in pieces:
        steps = jnp.exp(jax.random.uniform(jax.random.fold_in(own, axis_at), (parts,), jnp.float32, smallest / len(pieces), top_value / len(pieces)))
        level = level * jnp.repeat(steps, shape[axis_at] // parts).reshape([-1 if axis == axis_at else 1 for axis in range(len(shape))])
    return level


def bell_draw(rng, extent, spread, bound, shards=(), kind=jnp.bfloat16):
    drawn = spread * jax.random.normal(rng, extent, jnp.float32)
    if shards:
        drawn = drawn * level_of(rng, extent, shards, -0.22, 0.18)
    return jnp.clip(drawn, -bound, bound).astype(kind)


def setup_inputs(seed: int = 0, part: int = 0) -> dict:
    splits = jax.random.split(jax.random.key(seed), 12)
    part_keys = jax.random.split(jax.random.fold_in(splits[11], part), 12)
    queries = draw_queries(jax.random.fold_in(jax.random.fold_in(splits[11], part), 71), part)
    latent_cache = draw_latent_cache(jax.random.fold_in(jax.random.fold_in(splits[11], part), 71), part)
    lengths = draw_lengths(jax.random.fold_in(jax.random.fold_in(splits[11], part), 71), part)
    occupied = set_ends((jax.random.randint(part_keys[3], (SLOTS,), 0, 4) < 3).astype(jnp.int32), jax.random.fold_in(part_keys[3], 1), 0, 1)
    residual = bell_draw(part_keys[4], (SLOTS, D), 0.25, 4.0, ((0, 32),))
    w_uv = bell_draw(splits[5], (HEADS, LAT, VHEAD), LAT ** -0.5, 0.25, ((0, 32),))
    w_out = bell_draw(splits[6], (HEADS * VHEAD, D), (HEADS * VHEAD) ** -0.5, 0.046875, ((0, 32),))
    norm_gain = jnp.clip(1.0 + 0.1 * jax.random.normal(splits[7], (D,), jnp.float32), 0.5, 1.5).astype(jnp.bfloat16)
    w_gate = bell_draw(splits[8], (D, FF), D ** -0.5, 0.09375, ((1, 32),))
    w_up = bell_draw(splits[9], (D, FF), D ** -0.5, 0.09375, ((1, 32),))
    w_down = bell_draw(splits[10], (FF, D), FF ** -0.5, 0.0625, ((0, 32),))
    return {"queries": queries, "latent_cache": latent_cache, "lengths": lengths, "occupied": occupied, "residual": residual, "w_uv": w_uv, "w_out": w_out, "norm_gain": norm_gain, "w_gate": w_gate, "w_up": w_up, "w_down": w_down}


softmax_scale = 192.0 ** (-0.5)

def attend_slot(item):
    query, cache, length, flag = item
    scores = jnp.dot(query.astype(jnp.float32), cache.astype(jnp.float32).T) * softmax_scale
    live = jnp.arange(cache.shape[0], dtype=jnp.int32) < length
    scores = jnp.where(live[None, :], scores, jnp.float32(-1e+30))
    peak = lax.optimization_barrier(jnp.max(scores, axis=1, keepdims=True))
    weights = jnp.where(live[None, :], jnp.exp(scores - peak), jnp.float32(0.0))
    probs = (weights / lax.optimization_barrier(jnp.sum(weights, axis=1, keepdims=True))).astype(jnp.bfloat16)
    result = jnp.dot(probs, cache[:, :LAT], preferred_element_type=jnp.float32)
    return (result * flag.astype(jnp.float32)).astype(jnp.bfloat16)

def reference(queries, latent_cache, lengths, occupied, residual, w_uv, w_out, norm_gain, w_gate, w_up, w_down):
    latent_out = lax.map(attend_slot, (queries, latent_cache, lengths, occupied))
    values = jnp.einsum('shc,hcv->shv', latent_out.astype(jnp.float32), w_uv.astype(jnp.float32)).astype(jnp.bfloat16)
    attended = jnp.dot(values.reshape(SLOTS, HEADS * VHEAD), w_out, preferred_element_type=jnp.float32)
    hidden = (residual.astype(jnp.float32) + attended).astype(jnp.bfloat16)
    hidden_f = hidden.astype(jnp.float32)
    inverse = lax.rsqrt(lax.optimization_barrier(jnp.mean(hidden_f * hidden_f, axis=1, keepdims=True)) + 1e-06)
    normed = (hidden_f * inverse * norm_gain.astype(jnp.float32)).astype(jnp.bfloat16)
    gate = jnp.dot(normed, w_gate, preferred_element_type=jnp.float32)
    upper = jnp.dot(normed, w_up, preferred_element_type=jnp.float32)
    act = (jax.nn.silu(gate) * upper).astype(jnp.bfloat16)
    ffn = jnp.dot(act, w_down, preferred_element_type=jnp.float32)
    return (hidden_f + ffn).astype(jnp.bfloat16)
```

```python
import functools

import jax
import jax.numpy as jnp
from jax import lax
from jax.experimental import pallas as pl
from jax.experimental.pallas import tpu as pltpu
from jax.sharding import PartitionSpec as P

MESH = pl.DeviceIdType.MESH
F32 = jnp.float32
BF16 = jnp.bfloat16
softmax_scale = 192.0 ** (-0.5)

SIDE = 4
CHIPS = SIDE * SIDE
DEVICES = 2 * CHIPS
SLOT = 8
HEADS = 128
OWN_HEADS = HEADS // DEVICES
LAT = 512
KEY = 576
LMAX = 384
D = 3584
HALF = D // 2
PART = HALF // 2
ROWS = DEVICES * SLOT
FFS = 288
NT = (((1,), (1,)), ((), ()))
TN = (((0,), (0,)), ((), ()))


def remote(src, dst, send, recv, to):
    return pltpu.make_async_remote_copy(
        src_ref=src,
        dst_ref=dst,
        send_sem=send,
        recv_sem=recv,
        device_id={"wide": to},
        device_id_type=MESH,
    )


def layer_kernel(
    lengths,
    occupied,
    queries,
    cache,
    w_uv,
    w_out,
    w_gate,
    w_up,
    w_down,
    residual,
    gain,
    out,
    q_v,
    c_v,
    uv_v,
    wo_v,
    gu_v,
    wd_v,
    load_sem,
    attn,
    a2a_out,
    a2a_in,
    a2a_send,
    a2a_recv,
    rowvals,
    values,
    acc,
    p0,
    r0,
    s0,
    r1,
    s1,
    r2,
    rs_send,
    rs_recv,
    res_own,
    res16,
    hid,
    sq_own,
    sq_in,
    gathered,
    ag_send,
    ag_recv,
    last_own,
    last_in,
    pair_send,
    pair_recv,
):
    me = lax.axis_index("wide")
    core = lax.rem(me, 2)
    chip = me // 2
    x = lax.rem(chip, SIDE)
    y = chip // SIDE
    partner = me + 1 - 2 * core

    def at(cy, cx):
        return (cy * SIDE + cx) * 2 + core

    def along_x(k):
        return lax.rem(x + k, SIDE)

    def along_y(k):
        return lax.rem(y + k, SIDE)

    loads = []

    def load(src, dst):
        copy = pltpu.make_async_copy(src, dst, load_sem.at[len(loads)])
        copy.start()
        loads.append(copy)
        return copy

    slot_loads = []
    for s in range(SLOT):
        slot_loads.append((load(queries.at[s], q_v.at[s]), load(cache.at[s], c_v.at[s])))
    uv_loads = [
        load(w_uv.at[h], uv_v.at[:, pl.ds(h * 128, 128)]) for h in range(OWN_HEADS)
    ]
    wo_loads = [load(w_out.at[:, pl.ds(j * HALF, HALF)], wo_v.at[j]) for j in range(2)]
    gu_loads = [
        load(w_gate, gu_v.at[pl.ds(0, FFS)]),
        load(w_up, gu_v.at[pl.ds(FFS, FFS)]),
    ]
    wd_loads = [load(w_down.at[:, pl.ds(j * HALF, HALF)], wd_v.at[j]) for j in range(2)]

    barrier = pltpu.get_barrier_semaphore()

    def greet(k, carry):
        pl.semaphore_signal(
            barrier, inc=1, device_id={"wide": lax.rem(me + k, DEVICES)}, device_id_type=MESH
        )
        return carry

    lax.fori_loop(1, DEVICES, greet, 0)

    position = lax.broadcasted_iota(jnp.int32, (HEADS, LMAX), 1)
    for s in range(SLOT):
        for copy in slot_loads[s]:
            copy.wait()
        keys = c_v[s]
        scores = lax.dot_general(q_v[s], keys, TN, preferred_element_type=F32)
        scores = jnp.where(position < lengths[s], scores, F32(-1e30))
        peak = jnp.max(scores, axis=1, keepdims=True)
        weights = jnp.exp((scores - peak) * F32(softmax_scale))
        flag = occupied[s].astype(F32)
        probs = (weights * (flag / jnp.sum(weights, axis=1, keepdims=True))).astype(BF16)
        result = lax.dot_general(probs, keys[:LAT], NT, preferred_element_type=F32)
        for lane in range(LAT // 128):
            attn[lane, s * HEADS : (s + 1) * HEADS, :] = result[:, lane * 128 : (lane + 1) * 128]

    def pack(d, carry):
        for pair in range(OWN_HEADS // 2):
            for lane in range(LAT // 128):
                rows = [
                    attn[lane, pl.ds(d * OWN_HEADS + 2 * pair + i, SLOT, stride=HEADS), :]
                    for i in range(2)
                ]
                a2a_out[d, 16 * pair : 16 * pair + 16, lane * 128 : (lane + 1) * 128] = (
                    jnp.concatenate(rows, axis=0).astype(BF16)
                )
        return carry

    lax.fori_loop(0, DEVICES, pack, 0)

    pl.semaphore_wait(barrier, DEVICES - 1)

    for j in range(2):
        res_own[j] = residual[:, j * HALF : (j + 1) * HALF].astype(F32)
    res_copy = remote(
        res_own.at[1 - core], res16.at[core], pair_send.at[0], pair_recv.at[0], partner
    )
    res_copy.start()
    res16[core] = res_own[core]

    def a2a_copy(k):
        to = lax.rem(me + k, DEVICES)
        return remote(a2a_out.at[to], a2a_in.at[me], a2a_send.at[k], a2a_recv.at[k], to)

    def a2a_start(k, carry):
        a2a_copy(k).start()
        return carry

    lax.fori_loop(1, DEVICES, a2a_start, 0)
    a2a_in[me] = a2a_out[me]
    for copy in uv_loads + wo_loads:
        copy.wait()

    def a2a_wait(k, carry):
        a2a_copy(k).wait()
        return carry

    lax.fori_loop(1, DEVICES, a2a_wait, 0)

    rowvals[...] = jnp.dot(
        a2a_in[...].reshape(DEVICES * OWN_HEADS * SLOT, LAT), uv_v[...], preferred_element_type=F32
    ).reshape(DEVICES, OWN_HEADS * SLOT, OWN_HEADS * 128)
    for h in range(OWN_HEADS):
        mine = rowvals[:, h * SLOT : (h + 1) * SLOT, h * 128 : (h + 1) * 128]
        values[:, h * 128 : (h + 1) * 128] = mine.reshape(ROWS, 128).astype(BF16)

    def reduce_scatter(n, product):
        theirs = product(1 - core)
        p0[n] = theirs.astype(BF16).reshape(CHIPS, 16, HALF)
        first = remote(p0.at[n], r0.at[n], rs_send.at[n, 0], rs_recv.at[n, 0], partner)
        first.start()
        acc[...] = product(core).reshape(CHIPS, 16, HALF)
        first.wait()

        def add(d, carry):
            s0[n, d // SIDE, lax.rem(d, SIDE)] = (acc[d] + r0[n, d].astype(F32)).astype(BF16)
            return carry

        lax.fori_loop(0, CHIPS, add, 0)
        copies = []
        for k in (1, 3, 2):
            copies.append(
                remote(
                    s0.at[n, :, along_x(k), :, pl.ds(0, PART)],
                    r1.at[n, 0, k - 1],
                    rs_send.at[n, k],
                    rs_recv.at[n, k],
                    at(y, along_x(k)),
                )
            )
            copies.append(
                remote(
                    s0.at[n, along_y(k), :, :, pl.ds(PART, PART)],
                    r1.at[n, 1, k - 1],
                    rs_send.at[n, 3 + k],
                    rs_recv.at[n, 3 + k],
                    at(along_y(k), x),
                )
            )
        for copy in copies:
            copy.start()
        for copy in copies:
            copy.wait()
        for part in range(2):
            for i in range(SIDE):
                if part == 0:
                    total = s0[n, i, x, :, :PART]
                else:
                    total = s0[n, y, i, :, PART:]
                total = total.astype(F32)
                for k in range(3):
                    total += r1[n, part, k, i].astype(F32)
                s1[n, part, i] = total.astype(BF16)
        copies = []
        for k in (1, 3, 2):
            copies.append(
                remote(
                    s1.at[n, 0, along_y(k)],
                    r2.at[n, 0, k - 1],
                    rs_send.at[n, 6 + k],
                    rs_recv.at[n, 6 + k],
                    at(along_y(k), x),
                )
            )
            copies.append(
                remote(
                    s1.at[n, 1, along_x(k)],
                    r2.at[n, 1, k - 1],
                    rs_send.at[n, 9 + k],
                    rs_recv.at[n, 9 + k],
                    at(y, along_x(k)),
                )
            )
        for copy in copies:
            copy.start()
        for copy in copies:
            copy.wait()
        sums = []
        for part, own in ((0, y), (1, x)):
            total = s1[n, part, own].astype(F32)
            for k in range(3):
                total += r2[n, part, k].astype(F32)
            sums.append(total)
        return sums

    def attend(j):
        return jnp.dot(values[...], wo_v[j], preferred_element_type=F32)

    attended = reduce_scatter(0, attend)
    res_copy.wait()
    square = jnp.zeros((16, 1), F32)
    for part in range(2):
        mine = res16[:, :, part * PART : (part + 1) * PART].reshape(16, PART) + attended[part]
        mine = mine.astype(BF16).astype(F32)
        hid[:, part * PART : (part + 1) * PART] = mine
        square += jnp.sum(mine * mine, axis=1, keepdims=True)
    sq_own[...] = jnp.broadcast_to(square, (16, 128))
    sq_copy = remote(sq_own, sq_in, pair_send.at[1], pair_recv.at[1], partner)
    sq_copy.start()
    sq_copy.wait()
    inverse = lax.rsqrt((sq_own[:, :1] + sq_in[:, :1]) * F32(1.0 / D) + F32(1e-6))
    scaled = gain[:, pl.ds(pl.multiple_of(core * HALF, 128), HALF)].astype(F32)
    gathered[core, y, x] = (hid[...] * inverse * scaled).astype(BF16)

    def lanes(part):
        return pl.ds(part * PART, PART)

    copies = []
    for k in (1, 3, 2):
        for part, to in ((0, at(along_y(k), x)), (1, at(y, along_x(k)))):
            place = gathered.at[core, y, x, :, lanes(part)]
            copies.append(
                remote(place, place, ag_send.at[3 * part + k], ag_recv.at[3 * part + k], to)
            )
    for copy in copies:
        copy.start()
    for copy in copies:
        copy.wait()
    copies = []
    for k in (1, 3, 2):
        place = gathered.at[core, :, x, :, lanes(0)]
        copies.append(
            remote(place, place, ag_send.at[6 + k], ag_recv.at[6 + k], at(y, along_x(k)))
        )
        place = gathered.at[core, y, :, :, lanes(1)]
        copies.append(
            remote(place, place, ag_send.at[9 + k], ag_recv.at[9 + k], at(along_y(k), x))
        )
    for copy in copies:
        copy.start()
    for copy in copies:
        copy.wait()
    swap = remote(gathered.at[core], gathered.at[core], ag_send.at[0], ag_recv.at[0], partner)
    swap.start()
    for copy in gu_loads + wd_loads:
        copy.wait()

    def expand(j):
        return lax.dot_general(
            gu_v[:, pl.ds(pl.multiple_of(j * HALF, 128), HALF)],
            gathered[j].reshape(ROWS, HALF),
            NT,
            preferred_element_type=F32,
        )

    up = expand(core)
    swap.wait()
    up = up + expand(1 - core)
    gate = up[:FFS]
    act = (gate / (1.0 + jnp.exp(-gate)) * up[FFS:]).astype(BF16)

    def contract(j):
        return lax.dot_general(act, wd_v[j], TN, preferred_element_type=F32)

    ffn = reduce_scatter(1, contract)
    for part in range(2):
        total = hid[:, part * PART : (part + 1) * PART] + ffn[part]
        last_own[:, :, part * PART : (part + 1) * PART] = total.reshape(2, SLOT, PART)
    last = remote(last_own.at[1 - core], last_in, pair_send.at[2], pair_recv.at[2], partner)
    last.start()
    last.wait()
    out[:, pl.ds(pl.multiple_of(core * HALF, 128), HALF)] = last_own[core].astype(BF16)
    out[:, pl.ds(pl.multiple_of((1 - core) * HALF, 128), HALF)] = last_in[...].astype(BF16)


def shards(
    queries, latent_cache, lengths, occupied, residual, w_uv, w_out, norm_gain, w_gate, w_up, w_down
):
    hbm = pl.BlockSpec(memory_space=pl.ANY)
    vmem = pl.BlockSpec(memory_space=pltpu.VMEM)
    smem = pl.BlockSpec(memory_space=pltpu.SMEM)
    dma = pltpu.SemaphoreType.DMA
    return pl.pallas_call(
        layer_kernel,
        out_shape=jax.ShapeDtypeStruct((SLOT, D), BF16),
        in_specs=[smem, smem, hbm, hbm, hbm, hbm, hbm, hbm, hbm, vmem, vmem],
        out_specs=vmem,
        scratch_shapes=[
            pltpu.VMEM((SLOT, KEY, HEADS), BF16),
            pltpu.VMEM((SLOT, KEY, LMAX), BF16),
            pltpu.VMEM((LAT, OWN_HEADS * 128), BF16),
            pltpu.VMEM((2, OWN_HEADS * 128, HALF), BF16),
            pltpu.VMEM((2 * FFS, D), BF16),
            pltpu.VMEM((2, FFS, HALF), BF16),
            dma((2 * SLOT + OWN_HEADS + 6,)),
            pltpu.VMEM((LAT // 128, SLOT * HEADS, 128), F32),
            pltpu.VMEM((DEVICES, OWN_HEADS * SLOT, LAT), BF16),
            pltpu.VMEM((DEVICES, OWN_HEADS * SLOT, LAT), BF16),
            dma((DEVICES,)),
            dma((DEVICES,)),
            pltpu.VMEM((DEVICES, OWN_HEADS * SLOT, OWN_HEADS * 128), F32),
            pltpu.VMEM((ROWS, OWN_HEADS * 128), BF16),
            pltpu.VMEM((CHIPS, 16, HALF), F32),
            pltpu.VMEM((2, CHIPS, 16, HALF), BF16),
            pltpu.VMEM((2, CHIPS, 16, HALF), BF16),
            pltpu.VMEM((2, SIDE, SIDE, 16, HALF), BF16),
            pltpu.VMEM((2, 2, 3, SIDE, 16, PART), BF16),
            pltpu.VMEM((2, 2, SIDE, 16, PART), BF16),
            pltpu.VMEM((2, 2, 3, 16, PART), BF16),
            dma((2, 13)),
            dma((2, 13)),
            pltpu.VMEM((2, SLOT, HALF), F32),
            pltpu.VMEM((2, SLOT, HALF), F32),
            pltpu.VMEM((16, HALF), F32),
            pltpu.VMEM((16, 128), F32),
            pltpu.VMEM((16, 128), F32),
            pltpu.VMEM((2, SIDE, SIDE, 16, HALF), BF16),
            dma((13,)),
            dma((13,)),
            pltpu.VMEM((2, SLOT, HALF), F32),
            pltpu.VMEM((SLOT, HALF), F32),
            dma((3,)),
            dma((3,)),
        ],
        compiler_params=pltpu.CompilerParams(
            collective_id=0, has_side_effects=True, vmem_limit_bytes=60 * 2**20
        ),
        cost_estimate=pl.CostEstimate(
            flops=3_600_000_000, bytes_accessed=15_000_000, transcendentals=500_000
        ),
    )(
        lengths,
        occupied,
        jnp.swapaxes(queries, 1, 2),
        jnp.swapaxes(latent_cache, 1, 2),
        w_uv,
        w_out,
        w_gate.T,
        w_up.T,
        w_down,
        residual,
        norm_gain.reshape(1, D),
    )


def solution(mesh):
    in_specs = (
        P(("rep", "wide"), None, None),
        P(("rep", "wide"), None, None),
        P(("rep", "wide")),
        P(("rep", "wide")),
        P(("rep", "wide"), None),
        P("wide", None, None),
        P("wide", None),
        P(),
        P(None, "wide"),
        P(None, "wide"),
        P("wide", None),
    )
    out_specs = P(("rep", "wide"), None)
    return jax.shard_map(shards, mesh=mesh, in_specs=in_specs, out_specs=out_specs, check_vma=False)
```

```python
import jax
import jax.numpy as jnp
from jax import lax
from jax.experimental import pallas as pl
from jax.experimental.pallas import tpu as pltpu
from jax.sharding import PartitionSpec as P

MESH = pl.DeviceIdType.MESH
F32 = jnp.float32
BF16 = jnp.bfloat16
softmax_scale = 192.0 ** (-0.5)

SIDE = 4
CHIPS = SIDE * SIDE
DEVICES = 2 * CHIPS
SLOT = 8
WAVE = SLOT // 2
HEADS = 128
OWN_HEADS = HEADS // DEVICES
LAT = 512
LANES = LAT // 128
KEY = 576
LMAX = 384
D = 3584
HALF = D // 2
PART = HALF // 2
ROWS = DEVICES * WAVE
FFS = 288
NT = (((1,), (1,)), ((), ()))
TN = (((0,), (0,)), ((), ()))


def hops(offset):
    return sum(min(step, SIDE - step) for step in offset[:2])


OFFSETS = sorted(
    [(dy, dx, dc) for dy in range(SIDE) for dx in range(SIDE) for dc in range(2)][1:],
    key=lambda offset: -hops(offset),
)


def remote(src, dst, send, recv, to):
    return pltpu.make_async_remote_copy(
        src_ref=src,
        dst_ref=dst,
        send_sem=send,
        recv_sem=recv,
        device_id={"wide": to},
        device_id_type=MESH,
    )


def layer_kernel(
    lengths_hbm,
    occupied_hbm,
    queries,
    cache,
    w_uv,
    w_out,
    w_gate,
    w_up,
    w_down,
    residual_hbm,
    gain_hbm,
    out,
    lengths,
    occupied,
    residual,
    gain,
    gain_rows,
    scaled,
    q_v,
    c_v,
    uv_v,
    wo_v,
    gu_v,
    wd_v,
    load_sem,
    attn,
    a2a_out,
    a2a_in,
    a2a_send,
    a2a_recv,
    rowvals,
    values,
    acc,
    p0,
    r0,
    s0,
    r1,
    s1,
    r2,
    mine,
    rs_send,
    rs_recv,
    res_own,
    res_both,
    hid,
    sq_own,
    sq_in,
    gathered,
    ag_send,
    ag_recv,
    swap_send,
    swap_recv,
    up_own,
    acts,
    ends,
    last_own,
    last_in,
    pair_send,
    pair_recv,
):
    me = lax.axis_index("wide")
    core = lax.rem(me, 2)
    chip = me // 2
    x = lax.rem(chip, SIDE)
    y = chip // SIDE
    partner = me + 1 - 2 * core

    def at(cy, cx):
        return (cy * SIDE + cx) * 2 + core

    def along_x(k):
        return lax.rem(x + k, SIDE)

    def along_y(k):
        return lax.rem(y + k, SIDE)

    loads = []

    def load(src, dst):
        copy = pltpu.make_async_copy(src, dst, load_sem.at[len(loads)])
        copy.start()
        loads.append(copy)
        return copy

    count_loads = [load(lengths_hbm, lengths), load(occupied_hbm, occupied)]
    slot_loads = []
    for s in range(SLOT):
        slot_loads.append((load(queries.at[s], q_v.at[s]), load(cache.at[s], c_v.at[s])))

    barrier = pltpu.get_barrier_semaphore()

    def greet(k, carry):
        pl.semaphore_signal(
            barrier, inc=1, device_id={"wide": lax.rem(me + k, DEVICES)}, device_id_type=MESH
        )
        return carry

    lax.fori_loop(1, DEVICES, greet, 0)
    row_loads = [load(residual_hbm, residual), load(gain_hbm, gain)]
    uv_loads = [load(w_uv.at[h], uv_v.at[:, pl.ds(h * 128, 128)]) for h in range(OWN_HEADS)]
    wo_loads = [load(w_out.at[:, pl.ds(j * HALF, HALF)], wo_v.at[j]) for j in range(2)]
    gu_loads = [
        load(w_gate, gu_v.at[pl.ds(0, FFS)]),
        load(w_up, gu_v.at[pl.ds(FFS, FFS)]),
    ]
    wd_loads = [load(w_down.at[:, pl.ds(j * HALF, HALF)], wd_v.at[j]) for j in range(2)]

    def lanes(part):
        return pl.ds(part * PART, PART)

    def upper(rows):
        return lax.broadcasted_iota(jnp.int32, rows.shape, 0) < WAVE

    def stack(rows, more):
        return jnp.where(upper(rows), rows, pltpu.roll(more, WAVE, 0))

    def stack_last(rows, more):
        return jnp.where(upper(rows), pltpu.roll(rows, WAVE, 0), more)

    position = lax.broadcasted_iota(jnp.int32, (HEADS, LMAX), 1)

    def attend(w):
        for i in range(WAVE):
            s = w * WAVE + i
            for copy in slot_loads[s]:
                copy.wait()
            keys = c_v[s]
            scores = lax.dot_general(q_v[s], keys, TN, preferred_element_type=F32)
            scores = jnp.where(position < lengths[s], scores, F32(-1e30))
            peak = jnp.max(scores, axis=1, keepdims=True)
            weights = jnp.exp((scores - peak) * F32(softmax_scale))
            flag = occupied[s].astype(F32)
            probs = (weights * (flag / jnp.sum(weights, axis=1, keepdims=True))).astype(BF16)
            result = lax.dot_general(probs, keys[:LAT], NT, preferred_element_type=F32)
            for lane in range(LANES):
                attn[lane, i] = result[:, lane * 128 : (lane + 1) * 128]

        def pack(t, carry):
            for lane in range(LANES):
                tile = [attn[lane, i, pl.ds(pl.multiple_of(8 * t, 8), 8)] for i in range(WAVE)]
                for odd, join in enumerate((stack, stack_last)):
                    rows = jnp.concatenate([join(tile[0], tile[1]), join(tile[2], tile[3])], axis=0)
                    a2a_out[w, 2 * t + odd, :, lane * 128 : (lane + 1) * 128] = rows.astype(BF16)
            return carry

        lax.fori_loop(0, DEVICES // 2, pack, 0)

    def exchange(w):
        copies = []
        for k, (dy, dx, dc) in enumerate(OFFSETS):
            to = (along_y(dy) * SIDE + along_x(dx)) * 2 + lax.rem(core + dc, 2)
            copies.append(
                remote(
                    a2a_out.at[w, to],
                    a2a_in.at[w, me],
                    a2a_send.at[w, k],
                    a2a_recv.at[w, k],
                    to,
                )
            )
            copies[-1].start()
        a2a_in[w, me] = a2a_out[w, me]
        return copies

    def project(w, copies):
        for copy in copies:
            copy.wait()
        product = jnp.dot(
            a2a_in[w].reshape(DEVICES * OWN_HEADS * WAVE, LAT),
            uv_v[...],
            preferred_element_type=F32,
        )
        for h in range(OWN_HEADS):
            rowvals[h] = product[:, h * 128 : (h + 1) * 128]
        for h in range(OWN_HEADS):
            values[w, :, h * 128 : (h + 1) * 128] = rowvals[
                h, pl.ds(h, ROWS, stride=OWN_HEADS), :
            ].astype(BF16)

    def sum_pair(n, w, product):
        m = 2 * n + w
        p0[m] = product(1 - core).reshape(CHIPS, 8, HALF).astype(BF16)
        copy = remote(p0.at[m], r0.at[m], rs_send.at[m, 0], rs_recv.at[m, 0], partner)
        copy.start()
        acc[w] = product(core).reshape(SIDE, SIDE, 8, HALF)
        return [copy]

    def sum_first(n, w, copies):
        m = 2 * n + w
        for copy in copies:
            copy.wait()
        copies = []

        def place(part, k, i):
            return (i, along_x(k)) if part == 0 else (along_y(k), i)

        def added(part, k, i):
            cy, cx = place(part, k, i)
            block = (cy, cx, slice(None), slice(part * PART, (part + 1) * PART))
            return block, acc[(w, *block)] + r0[m, cy * SIDE + cx, :, block[3]].astype(F32)

        for k in (2, 1, 3):
            for part in range(2):
                for i in range(SIDE):
                    block, total = added(part, k, i)
                    s0[(m, *block)] = total.astype(BF16)
                copies.append(
                    remote(
                        s0.at[m, :, along_x(k), :, lanes(0)]
                        if part == 0
                        else s0.at[m, along_y(k), :, :, lanes(1)],
                        r1.at[m, part, k - 1],
                        rs_send.at[m, 3 * part + k],
                        rs_recv.at[m, 3 * part + k],
                        at(y, along_x(k)) if part == 0 else at(along_y(k), x),
                    )
                )
                copies[-1].start()
        for part in range(2):
            for i in range(SIDE):
                block, total = added(part, 0, i)
                acc[(w, *block)] = total
        return copies

    def sum_second(n, w, copies):
        m = 2 * n + w
        later = []
        for part in range(2):
            for copy in copies[part::2]:
                copy.wait()
            for k in (2, 1, 3, 0):
                to = along_y(k) if part == 0 else along_x(k)
                if part == 0:
                    total = acc[w, to, x, :, :PART]
                else:
                    total = acc[w, y, to, :, PART:]
                for i in range(3):
                    total += r1[m, part, i, to].astype(F32)
                if k == 0:
                    mine[w, :, part * PART : (part + 1) * PART] = total
                else:
                    s1[m, part, to] = total.astype(BF16)
                    later.append(
                        remote(
                            s1.at[m, part, to],
                            r2.at[m, part, k - 1],
                            rs_send.at[m, 6 + 3 * part + k],
                            rs_recv.at[m, 6 + 3 * part + k],
                            at(to, x) if part == 0 else at(y, to),
                        )
                    )
                    later[-1].start()
        return later

    def sum_last(n, w, copies):
        m = 2 * n + w
        for copy in copies:
            copy.wait()
        sums = []
        for part in range(2):
            total = mine[w, :, part * PART : (part + 1) * PART]
            for i in range(3):
                total += r2[m, part, i].astype(F32)
            sums.append(total)
        return sums

    def hide(w, copies):
        sums = sum_last(0, w, copies)
        if w == 0:
            res_copy.wait()
        square = jnp.zeros((8, 1), F32)
        for part in range(2):
            columns = slice(part * PART, (part + 1) * PART)
            join = stack if w == 0 else stack_last
            rows = join(res_both[0, :, columns], res_both[1, :, columns]) + sums[part]
            rows = rows.astype(BF16).astype(F32)
            hid[w, :, columns] = rows
            square += jnp.sum(rows * rows, axis=1, keepdims=True)
        sq_own[w] = jnp.broadcast_to(square, (8, 128))
        copy = remote(
            sq_own.at[w], sq_in.at[w], pair_send.at[1 + w], pair_recv.at[1 + w], partner
        )
        copy.start()
        return [copy]

    def gather_first(w, copies):
        copies[0].wait()
        inverse = lax.rsqrt((sq_own[w, :, :1] + sq_in[w, :, :1]) * F32(1.0 / D) + F32(1e-6))
        gathered[w, core, y, x] = (hid[w] * inverse * scaled[...]).astype(BF16)
        copies = []
        for k in (2, 1, 3):
            for part, to in ((0, at(along_y(k), x)), (1, at(y, along_x(k)))):
                place = gathered.at[w, core, y, x, :, lanes(part)]
                copies.append(
                    remote(
                        place,
                        place,
                        ag_send.at[w, 3 * part + k],
                        ag_recv.at[w, 3 * part + k],
                        to,
                    )
                )
                copies[-1].start()
        return copies

    def column(w, part, k):
        if part == 0:
            return gathered.at[w, core, :, along_x(k), :, lanes(0)]
        return gathered.at[w, core, along_y(k), :, :, lanes(1)]

    def swap(w, part, k):
        place = column(w, part, k)
        copy = remote(
            place, place, swap_send.at[w, part, k], swap_recv.at[w, part, k], partner
        )
        copy.start()
        return copy

    def gather_second(w, copies):
        for copy in copies:
            copy.wait()
        copies = []
        for k in (2, 1, 3):
            for part, to in ((0, at(y, along_x(k))), (1, at(along_y(k), x))):
                place = column(w, part, 0)
                copies.append(
                    remote(
                        place,
                        place,
                        ag_send.at[w, 6 + 3 * part + k],
                        ag_recv.at[w, 6 + 3 * part + k],
                        to,
                    )
                )
                copies[-1].start()
        return copies, [swap(w, 0, 0), swap(w, 1, 0)]

    def forward(w, state):
        copies, swaps = state
        for i, k in ((2, 1), (4, 3), (0, 2)):
            for part in range(2):
                copies[i + part].wait()
                swaps.append(swap(w, part, SIDE - k))
        return swaps

    def wide(w, j):
        rows = gathered[w, j].astype(F32).reshape(ROWS, HALF).astype(BF16)
        return lax.dot_general(
            gu_v[:, pl.ds(pl.multiple_of(j * HALF, 128), HALF)],
            rows,
            NT,
            preferred_element_type=F32,
        )

    def expand_own(w):
        up_own[w] = wide(w, core)

    def expand(w, swaps):
        for copy in swaps:
            copy.wait()
        up = up_own[w] + wide(w, 1 - core)
        gate = up[:FFS]
        acts[w] = (gate / (1.0 + jnp.exp(-gate)) * up[FFS:]).astype(BF16)

    def inward(w):
        return lambda j: lax.dot_general(acts[w], wd_v[j], TN, preferred_element_type=F32)

    def finish(w, copies):
        sums = sum_last(1, w, copies)
        for part in range(2):
            columns = slice(part * PART, (part + 1) * PART)
            ends[w, :, columns] = hid[w, :, columns] + sums[part]

    for copy in count_loads:
        copy.wait()
    attend(0)
    pl.semaphore_wait(barrier, DEVICES - 1)
    sent0 = exchange(0)
    for copy in row_loads:
        copy.wait()
    for j in range(2):
        res_own[j] = residual[:, j * HALF : (j + 1) * HALF].astype(F32)
    res_copy = remote(
        res_own.at[1 - core], res_both.at[core], pair_send.at[0], pair_recv.at[0], partner
    )
    res_copy.start()
    res_both[core] = res_own[core]
    attend(1)
    sent1 = exchange(1)
    gain_rows[...] = gain[...].astype(F32)
    for t in range(HALF // 128):
        row = gain_rows[pl.ds(core * (HALF // 128) + t, 1), :]
        scaled[:, t * 128 : (t + 1) * 128] = jnp.broadcast_to(row, (8, 128))
    for copy in uv_loads + wo_loads:
        copy.wait()

    def outward(w):
        return lambda j: jnp.dot(values[w], wo_v[j], preferred_element_type=F32)

    project(0, sent0)
    step0 = sum_pair(0, 0, outward(0))
    step0 = sum_first(0, 0, step0)
    project(1, sent1)
    step1 = sum_pair(0, 1, outward(1))
    step0 = sum_second(0, 0, step0)
    step1 = sum_first(0, 1, step1)
    step0 = hide(0, step0)
    step0 = gather_first(0, step0)
    step1 = sum_second(0, 1, step1)
    step0 = gather_second(0, step0)
    for copy in gu_loads + wd_loads:
        copy.wait()
    step1 = hide(1, step1)
    step1 = gather_first(1, step1)
    step0 = forward(0, step0)
    expand_own(0)
    step1 = gather_second(1, step1)
    expand(0, step0)
    step0 = sum_pair(1, 0, inward(0))
    step0 = sum_first(1, 0, step0)
    step1 = forward(1, step1)
    expand_own(1)
    expand(1, step1)
    step1 = sum_pair(1, 1, inward(1))
    step0 = sum_second(1, 0, step0)
    step1 = sum_first(1, 1, step1)
    finish(0, step0)
    step1 = sum_second(1, 1, step1)
    finish(1, step1)
    last_own[0] = stack(ends[0], ends[1])
    last_own[1] = stack_last(ends[0], ends[1])
    last = remote(last_own.at[1 - core], last_in, pair_send.at[3], pair_recv.at[3], partner)
    last.start()
    last.wait()
    out[:, pl.ds(pl.multiple_of(core * HALF, 128), HALF)] = last_own[core].astype(BF16)
    out[:, pl.ds(pl.multiple_of((1 - core) * HALF, 128), HALF)] = last_in[...].astype(BF16)


def shards(
    queries, latent_cache, lengths, occupied, residual, w_uv, w_out, norm_gain, w_gate, w_up, w_down
):
    hbm = pl.BlockSpec(memory_space=pl.ANY)
    vmem = pl.BlockSpec(memory_space=pltpu.VMEM)
    dma = pltpu.SemaphoreType.DMA
    return pl.pallas_call(
        layer_kernel,
        out_shape=jax.ShapeDtypeStruct((SLOT, D), BF16),
        in_specs=[hbm] * 11,
        out_specs=vmem,
        scratch_shapes=[
            pltpu.SMEM((SLOT,), jnp.int32),
            pltpu.SMEM((SLOT,), jnp.int32),
            pltpu.VMEM((SLOT, D), BF16),
            pltpu.VMEM((D // 128, 128), BF16),
            pltpu.VMEM((D // 128, 128), F32),
            pltpu.VMEM((8, HALF), F32),
            pltpu.VMEM((SLOT, KEY, HEADS), BF16),
            pltpu.VMEM((SLOT, KEY, LMAX), BF16),
            pltpu.VMEM((LAT, OWN_HEADS * 128), BF16),
            pltpu.VMEM((2, OWN_HEADS * 128, HALF), BF16),
            pltpu.VMEM((2 * FFS, D), BF16),
            pltpu.VMEM((2, FFS, HALF), BF16),
            dma((2 * SLOT + OWN_HEADS + 10,)),
            pltpu.VMEM((LANES, WAVE, HEADS, 128), F32),
            pltpu.VMEM((2, DEVICES, OWN_HEADS * WAVE, LAT), BF16),
            pltpu.VMEM((2, DEVICES, OWN_HEADS * WAVE, LAT), BF16),
            dma((2, DEVICES)),
            dma((2, DEVICES)),
            pltpu.VMEM((OWN_HEADS, ROWS * OWN_HEADS, 128), F32),
            pltpu.VMEM((2, ROWS, OWN_HEADS * 128), BF16),
            pltpu.VMEM((2, SIDE, SIDE, 8, HALF), F32),
            pltpu.VMEM((4, CHIPS, 8, HALF), BF16),
            pltpu.VMEM((4, CHIPS, 8, HALF), BF16),
            pltpu.VMEM((4, SIDE, SIDE, 8, HALF), BF16),
            pltpu.VMEM((4, 2, 3, SIDE, 8, PART), BF16),
            pltpu.VMEM((4, 2, SIDE, 8, PART), BF16),
            pltpu.VMEM((4, 2, 3, 8, PART), BF16),
            pltpu.VMEM((2, 8, HALF), F32),
            dma((4, 13)),
            dma((4, 13)),
            pltpu.VMEM((2, SLOT, HALF), F32),
            pltpu.VMEM((2, SLOT, HALF), F32),
            pltpu.VMEM((2, 8, HALF), F32),
            pltpu.VMEM((2, 8, 128), F32),
            pltpu.VMEM((2, 8, 128), F32),
            pltpu.VMEM((2, 2, SIDE, SIDE, 8, HALF), BF16),
            dma((2, 13)),
            dma((2, 13)),
            dma((2, 2, SIDE)),
            dma((2, 2, SIDE)),
            pltpu.VMEM((2, 2 * FFS, ROWS), F32),
            pltpu.VMEM((2, FFS, ROWS), BF16),
            pltpu.VMEM((2, 8, HALF), F32),
            pltpu.VMEM((2, SLOT, HALF), F32),
            pltpu.VMEM((SLOT, HALF), F32),
            dma((4,)),
            dma((4,)),
        ],
        compiler_params=pltpu.CompilerParams(
            collective_id=0, has_side_effects=True, vmem_limit_bytes=60 * 2**20
        ),
        cost_estimate=pl.CostEstimate(
            flops=3_600_000_000, bytes_accessed=15_000_000, transcendentals=500_000
        ),
    )(
        lengths,
        occupied,
        jnp.swapaxes(queries, 1, 2),
        jnp.swapaxes(latent_cache, 1, 2),
        w_uv,
        w_out,
        w_gate.T,
        w_up.T,
        w_down,
        residual,
        norm_gain.reshape(D // 128, 128),
    )


def solution(mesh):
    in_specs = (
        P(("rep", "wide"), None, None),
        P(("rep", "wide"), None, None),
        P(("rep", "wide")),
        P(("rep", "wide")),
        P(("rep", "wide"), None),
        P("wide", None, None),
        P("wide", None),
        P(),
        P(None, "wide"),
        P(None, "wide"),
        P("wide", None),
    )
    out_specs = P(("rep", "wide"), None)
    return jax.shard_map(shards, mesh=mesh, in_specs=in_specs, out_specs=out_specs, check_vma=False)
```

```python
import jax
import jax.numpy as jnp
from jax import lax
from jax.experimental import pallas as pl
from jax.experimental.pallas import tpu as pltpu
from jax.sharding import PartitionSpec as P

MESH = pl.DeviceIdType.MESH
F32 = jnp.float32
BF16 = jnp.bfloat16
softmax_scale = 192.0 ** (-0.5)

SIDE = 4
CHIPS = SIDE * SIDE
DEVICES = 2 * CHIPS
SLOT = 8
WAVE = SLOT // 2
HEADS = 128
OWN_HEADS = HEADS // DEVICES
LAT = 512
LANES = LAT // 128
KEY = 576
LMAX = 384
D = 3584
HALF = D // 2
ROWS = DEVICES * WAVE
FFS = 288
NT = (((1,), (1,)), ((), ()))
TN = (((0,), (0,)), ((), ()))


def hops(offset):
    return sum(min(step, SIDE - step) for step in offset[:2])


CHIP_OFFSETS = sorted(
    [(dy, dx) for dy in range(SIDE) for dx in range(SIDE)][1:], key=lambda offset: -hops(offset)
)

OFFSETS = sorted(
    [(dy, dx, dc) for dy in range(SIDE) for dx in range(SIDE) for dc in range(2)][1:],
    key=lambda offset: -hops(offset),
)


def wait_bytes(ref, sem):
    pltpu.make_async_copy(ref, ref, sem).wait()


def remote(src, dst, send, recv, to):
    return pltpu.make_async_remote_copy(
        src_ref=src,
        dst_ref=dst,
        send_sem=send,
        recv_sem=recv,
        device_id={"wide": to},
        device_id_type=MESH,
    )


def layer_kernel(
    lengths_hbm,
    occupied_hbm,
    queries,
    cache,
    w_uv,
    w_out,
    w_gate,
    w_up,
    w_down,
    residual_hbm,
    gain_hbm,
    out,
    lengths,
    occupied,
    residual,
    gain,
    gain_rows,
    scaled,
    q_v,
    c_v,
    uv_v,
    wo_v,
    gu_v,
    wd_v,
    load_sem,
    attn,
    a2a_out,
    a2a_in,
    a2a_send,
    a2a_recv,
    rowvals,
    values,
    acc,
    s0,
    rd,
    pair_of_send,
    pair_of_recv,
    rd_send,
    rd_recv,
    res_own,
    res_both,
    hid,
    sq_own,
    sq_in,
    gathered,
    ag_send,
    ag_recv,
    swap_send,
    swap_recv,
    up_own,
    acts,
    ends,
    last_own,
    last_in,
    pair_send,
    pair_recv,
):
    me = lax.axis_index("wide")
    core = lax.rem(me, 2)
    chip = me // 2
    x = lax.rem(chip, SIDE)
    y = chip // SIDE
    partner = me + 1 - 2 * core

    def at(cy, cx):
        return (cy * SIDE + cx) * 2 + core

    def along_x(k):
        return lax.rem(x + k, SIDE)

    def along_y(k):
        return lax.rem(y + k, SIDE)

    loads = []

    def load(src, dst, same=0):
        copy = pltpu.make_async_copy(src, dst, load_sem.at[len(loads) - same])
        copy.start()
        if not same:
            loads.append(copy)
        return copy

    count_loads = [load(lengths_hbm, lengths), load(occupied_hbm, occupied)]
    query_loads = []
    cache_loads = []
    for w in range(2):
        wave = pl.ds(w * WAVE, WAVE)
        query_loads.append(load(queries.at[wave], q_v.at[wave]))
        if w == 0:
            cache_loads += [load(cache.at[s], c_v.at[s]) for s in range(WAVE)]
        else:
            cache_loads.append(load(cache.at[wave], c_v.at[wave]))

    barrier = pltpu.get_barrier_semaphore()

    def greet(k, carry):
        pl.semaphore_signal(
            barrier, inc=1, device_id={"wide": lax.rem(me + k, DEVICES)}, device_id_type=MESH
        )
        return carry

    lax.fori_loop(1, DEVICES, greet, 0)
    row_loads = [load(residual_hbm, residual), load(gain_hbm, gain)]
    for h in range(OWN_HEADS):
        load(w_uv.at[h], uv_v.at[:, pl.ds(h * 128, 128)], same=min(h, 1))
    uv_sem = load_sem.at[len(loads) - 1]
    own_half = pl.ds(pl.multiple_of(core * HALF, 128), HALF)
    wo_loads = [load(w_out.at[:, own_half], wo_v.at[core])]
    load(w_gate, gu_v.at[pl.ds(0, FFS)])
    load(w_up, gu_v.at[pl.ds(FFS, FFS)], same=1)
    gu_sem = load_sem.at[len(loads) - 1]
    wd_loads = [load(w_down.at[:, own_half], wd_v.at[core])]

    def upper(rows):
        return lax.broadcasted_iota(jnp.int32, rows.shape, 0) < WAVE

    def stack(rows, more):
        return jnp.where(upper(rows), rows, pltpu.roll(more, WAVE, 0))

    def stack_last(rows, more):
        return jnp.where(upper(rows), pltpu.roll(rows, WAVE, 0), more)

    position = lax.broadcasted_iota(jnp.int32, (HEADS, LMAX), 1)

    def attend(w):
        for i in range(WAVE):
            s = w * WAVE + i
            if i == 0:
                query_loads[w].wait()
            if s <= WAVE:
                cache_loads[s].wait()
            keys = c_v[s]
            scores = lax.dot_general(q_v[s], keys, TN, preferred_element_type=F32)
            scores = jnp.where(position < lengths[s], scores, F32(-1e30))
            peak = jnp.max(scores, axis=1, keepdims=True)
            weights = jnp.exp((scores - peak) * F32(softmax_scale))
            flag = occupied[s].astype(F32)
            probs = (weights * (flag / jnp.sum(weights, axis=1, keepdims=True))).astype(BF16)
            result = lax.dot_general(probs, keys[:LAT], NT, preferred_element_type=F32)
            for lane in range(LANES):
                attn[lane, i] = result[:, lane * 128 : (lane + 1) * 128]

        def pack(t, carry):
            for lane in range(LANES):
                tile = [attn[lane, i, pl.ds(pl.multiple_of(8 * t, 8), 8)] for i in range(WAVE)]
                for odd, join in enumerate((stack, stack_last)):
                    rows = jnp.concatenate([join(tile[0], tile[1]), join(tile[2], tile[3])], axis=0)
                    a2a_out[w, 2 * t + odd, :, lane * 128 : (lane + 1) * 128] = rows.astype(BF16)
            return carry

        lax.fori_loop(0, DEVICES // 2, pack, 0)

    def exchange(w):
        for dy, dx, dc in OFFSETS:
            to = (along_y(dy) * SIDE + along_x(dx)) * 2 + lax.rem(core + dc, 2)
            remote(
                a2a_out.at[w, to], a2a_in.at[w, me], a2a_send.at[w], a2a_recv.at[w], to
            ).start()
        a2a_in[w, me] = a2a_out[w, me]

    def project(w):
        others = a2a_in.at[w, pl.ds(0, DEVICES - 1)]
        wait_bytes(others, a2a_recv.at[w])
        wait_bytes(others, a2a_send.at[w])
        product = jnp.dot(
            a2a_in[w].reshape(DEVICES * OWN_HEADS * WAVE, LAT),
            uv_v[...],
            preferred_element_type=F32,
        )
        for h in range(OWN_HEADS):
            rowvals[h] = product[:, h * 128 : (h + 1) * 128]
        for h in range(OWN_HEADS):
            values[w, core, :, h * 128 : (h + 1) * 128] = rowvals[
                h, pl.ds(h, ROWS, stride=OWN_HEADS), :
            ].astype(BF16)

    def sum_pair(n, w, given, product):
        m = 2 * n + w
        place = given.at[w, core]
        copy = remote(place, place, pair_of_send.at[m], pair_of_recv.at[m], partner)
        copy.start()
        acc[w] = product(core).reshape(SIDE, SIDE, 8, HALF)
        copy.wait()
        acc[w] += product(1 - core).reshape(SIDE, SIDE, 8, HALF)

    def sum_start(n, w):
        m = 2 * n + w
        for i, (dy, dx) in enumerate(CHIP_OFFSETS):
            to = (along_y(dy), along_x(dx))
            s0[(m, *to)] = acc[(w, *to)].astype(BF16)
            remote(s0.at[(m, *to)], rd.at[m, i], rd_send.at[m], rd_recv.at[m], at(*to)).start()

    def sum_end(n, w):
        m = 2 * n + w
        wait_bytes(rd.at[m], rd_recv.at[m])
        wait_bytes(rd.at[m], rd_send.at[m])
        total = acc[w, y, x]
        for i in range(CHIPS - 1):
            total += rd[m, i].astype(F32)
        return total

    def hide(w):
        if w == 0:
            res_copy.wait()
        join = stack if w == 0 else stack_last
        rows = join(res_both[0], res_both[1]) + sum_end(0, w)
        rows = rows.astype(BF16).astype(F32)
        hid[w] = rows
        square = jnp.sum(rows * rows, axis=1, keepdims=True)
        sq_own[w] = jnp.broadcast_to(square, (8, 128))
        copy = remote(
            sq_own.at[w], sq_in.at[w], pair_send.at[1 + w], pair_recv.at[1 + w], partner
        )
        copy.start()
        return copy

    def gather(w, copy):
        copy.wait()
        inverse = lax.rsqrt((sq_own[w, :, :1] + sq_in[w, :, :1]) * F32(1.0 / D) + F32(1e-6))
        gathered[w, core, y, x] = (hid[w] * inverse * scaled[...]).astype(BF16)
        place = gathered.at[w, core, y, x]
        for dy, dx in CHIP_OFFSETS:
            to = at(along_y(dy), along_x(dx))
            remote(place, place, ag_send.at[w], ag_recv.at[w, dy], to).start()

    def forward(w):
        for dy in (2, 1, 3, 0):
            row = gathered.at[w, core, along_y((SIDE - dy) % SIDE)]
            wait_bytes(row.at[pl.ds(0, SIDE if dy else SIDE - 1)], ag_recv.at[w, dy])
            remote(row, row, swap_send.at[w], swap_recv.at[w], partner).start()

    def wide(w, j):
        rows = gathered[w, j].astype(F32).reshape(ROWS, HALF).astype(BF16)
        return lax.dot_general(
            gu_v[:, pl.ds(pl.multiple_of(j * HALF, 128), HALF)],
            rows,
            NT,
            preferred_element_type=F32,
        )

    def expand_own(w):
        up_own[w] = wide(w, core)

    def expand(w):
        wait_bytes(gathered.at[w, 1 - core], swap_recv.at[w])
        wait_bytes(gathered.at[w, 1 - core], swap_send.at[w])
        up = up_own[w] + wide(w, 1 - core)
        gate = up[:FFS]
        acts[w, core] = (gate / (1.0 + jnp.exp(-gate)) * up[FFS:]).astype(BF16)

    def inward(w):
        return lambda j: lax.dot_general(acts[w, j], wd_v[j], TN, preferred_element_type=F32)

    def finish(w):
        ends[w] = hid[w] + sum_end(1, w)

    for copy in count_loads:
        copy.wait()
    attend(0)
    pl.semaphore_wait(barrier, DEVICES - 1)
    exchange(0)
    for copy in row_loads:
        copy.wait()
    for j in range(2):
        res_own[j] = residual[:, j * HALF : (j + 1) * HALF].astype(F32)
    res_copy = remote(
        res_own.at[1 - core], res_both.at[core], pair_send.at[0], pair_recv.at[0], partner
    )
    res_copy.start()
    other_half = pl.ds(pl.multiple_of((1 - core) * HALF, 128), HALF)
    wo_copy = remote(
        w_out.at[:, other_half], wo_v.at[core], pair_send.at[4], pair_recv.at[4], partner
    )
    wd_copy = remote(
        w_down.at[:, other_half], wd_v.at[core], pair_send.at[5], pair_recv.at[5], partner
    )
    wo_copy.start()
    wd_copy.start()
    res_both[core] = res_own[core]
    attend(1)
    exchange(1)
    gain_rows[...] = gain[...].astype(F32)
    for t in range(HALF // 128):
        row = gain_rows[pl.ds(core * (HALF // 128) + t, 1), :]
        scaled[:, t * 128 : (t + 1) * 128] = jnp.broadcast_to(row, (8, 128))
    wait_bytes(uv_v, uv_sem)
    wo_loads[0].wait()

    def outward(w):
        return lambda j: jnp.dot(values[w, j], wo_v[j], preferred_element_type=F32)

    project(0)
    wo_copy.wait()
    sum_pair(0, 0, values, outward(0))
    sum_start(0, 0)
    project(1)
    sum_pair(0, 1, values, outward(1))
    sum_start(0, 1)
    square0 = hide(0)
    gather(0, square0)
    wait_bytes(gu_v, gu_sem)
    wd_loads[0].wait()
    wd_copy.wait()
    square1 = hide(1)
    gather(1, square1)
    forward(0)
    expand_own(0)
    expand(0)
    sum_pair(1, 0, acts, inward(0))
    sum_start(1, 0)
    forward(1)
    expand_own(1)
    expand(1)
    sum_pair(1, 1, acts, inward(1))
    sum_start(1, 1)
    finish(0)
    finish(1)
    last_own[0] = stack(ends[0], ends[1])
    last_own[1] = stack_last(ends[0], ends[1])
    last = remote(last_own.at[1 - core], last_in, pair_send.at[3], pair_recv.at[3], partner)
    last.start()
    for w in range(2):
        wait_bytes(gathered.at[w, core, pl.ds(0, SIDE - 1)], ag_send.at[w])
        wait_bytes(gathered.at[w, core, 0, pl.ds(0, SIDE - 1)], ag_send.at[w])
    last.wait()
    out[:, pl.ds(pl.multiple_of(core * HALF, 128), HALF)] = last_own[core].astype(BF16)
    out[:, pl.ds(pl.multiple_of((1 - core) * HALF, 128), HALF)] = last_in[...].astype(BF16)


def shards(
    queries, latent_cache, lengths, occupied, residual, w_uv, w_out, norm_gain, w_gate, w_up, w_down
):
    hbm = pl.BlockSpec(memory_space=pl.ANY)
    vmem = pl.BlockSpec(memory_space=pltpu.VMEM)
    dma = pltpu.SemaphoreType.DMA
    return pl.pallas_call(
        layer_kernel,
        out_shape=jax.ShapeDtypeStruct((SLOT, D), BF16),
        in_specs=[hbm] * 11,
        out_specs=vmem,
        scratch_shapes=[
            pltpu.SMEM((SLOT,), jnp.int32),
            pltpu.SMEM((SLOT,), jnp.int32),
            pltpu.VMEM((SLOT, D), BF16),
            pltpu.VMEM((D // 128, 128), BF16),
            pltpu.VMEM((D // 128, 128), F32),
            pltpu.VMEM((8, HALF), F32),
            pltpu.VMEM((SLOT, KEY, HEADS), BF16),
            pltpu.VMEM((SLOT, KEY, LMAX), BF16),
            pltpu.VMEM((LAT, OWN_HEADS * 128), BF16),
            pltpu.VMEM((2, OWN_HEADS * 128, HALF), BF16),
            pltpu.VMEM((2 * FFS, D), BF16),
            pltpu.VMEM((2, FFS, HALF), BF16),
            dma((15,)),
            pltpu.VMEM((LANES, WAVE, HEADS, 128), F32),
            pltpu.VMEM((2, DEVICES, OWN_HEADS * WAVE, LAT), BF16),
            pltpu.VMEM((2, DEVICES, OWN_HEADS * WAVE, LAT), BF16),
            dma((2,)),
            dma((2,)),
            pltpu.VMEM((OWN_HEADS, ROWS * OWN_HEADS, 128), F32),
            pltpu.VMEM((2, 2, ROWS, OWN_HEADS * 128), BF16),
            pltpu.VMEM((2, SIDE, SIDE, 8, HALF), F32),
            pltpu.VMEM((4, SIDE, SIDE, 8, HALF), BF16),
            pltpu.VMEM((4, CHIPS - 1, 8, HALF), BF16),
            dma((4,)),
            dma((4,)),
            dma((4,)),
            dma((4,)),
            pltpu.VMEM((2, SLOT, HALF), F32),
            pltpu.VMEM((2, SLOT, HALF), F32),
            pltpu.VMEM((2, 8, HALF), F32),
            pltpu.VMEM((2, 8, 128), F32),
            pltpu.VMEM((2, 8, 128), F32),
            pltpu.VMEM((2, 2, SIDE, SIDE, 8, HALF), BF16),
            dma((2,)),
            dma((2, SIDE)),
            dma((2,)),
            dma((2,)),
            pltpu.VMEM((2, 2 * FFS, ROWS), F32),
            pltpu.VMEM((2, 2, FFS, ROWS), BF16),
            pltpu.VMEM((2, 8, HALF), F32),
            pltpu.VMEM((2, SLOT, HALF), F32),
            pltpu.VMEM((SLOT, HALF), F32),
            dma((6,)),
            dma((6,)),
        ],
        compiler_params=pltpu.CompilerParams(
            collective_id=0, has_side_effects=True, vmem_limit_bytes=60 * 2**20
        ),
        cost_estimate=pl.CostEstimate(
            flops=3_600_000_000, bytes_accessed=15_000_000, transcendentals=500_000
        ),
    )(
        lengths,
        occupied,
        jnp.swapaxes(queries, 1, 2),
        jnp.swapaxes(latent_cache, 1, 2),
        w_uv,
        w_out,
        w_gate.T,
        w_up.T,
        w_down,
        residual,
        norm_gain.reshape(D // 128, 128),
    )


def solution(mesh):
    in_specs = (
        P(("rep", "wide"), None, None),
        P(("rep", "wide"), None, None),
        P(("rep", "wide")),
        P(("rep", "wide")),
        P(("rep", "wide"), None),
        P("wide", None, None),
        P("wide", None),
        P(),
        P(None, "wide"),
        P(None, "wide"),
        P("wide", None),
    )
    out_specs = P(("rep", "wide"), None)
    return jax.shard_map(shards, mesh=mesh, in_specs=in_specs, out_specs=out_specs, check_vma=False)
```

```python
import jax
import jax.numpy as jnp
from jax import lax
from jax.experimental import pallas as pl
from jax.experimental.pallas import tpu as pltpu
from jax.sharding import PartitionSpec as P

MESH = pl.DeviceIdType.MESH
F32 = jnp.float32
BF16 = jnp.bfloat16
softmax_scale = 192.0 ** (-0.5)

SIDE = 4
CHIPS = SIDE * SIDE
DEVICES = 2 * CHIPS
SLOT = 8
WAVE = SLOT // 2
HEADS = 128
OWN_HEADS = HEADS // DEVICES
LAT = 512
LANES = LAT // 128
KEY = 576
LMAX = 384
D = 3584
HALF = D // 2
ROWS = DEVICES * WAVE
FFS = 288
NT = (((1,), (1,)), ((), ()))
TN = (((0,), (0,)), ((), ()))


def hops(offset):
    return sum(min(step, SIDE - step) for step in offset[:2])


CHIP_OFFSETS = sorted(
    [(dy, dx) for dy in range(SIDE) for dx in range(SIDE)][1:], key=lambda offset: -hops(offset)
)

OFFSETS = sorted(
    [(dy, dx, dc) for dy in range(SIDE) for dx in range(SIDE) for dc in range(2)][1:],
    key=lambda offset: -hops(offset),
)


def wait_bytes(ref, sem):
    pltpu.make_async_copy(ref, ref, sem).wait()


def remote(src, dst, send, recv, to):
    return pltpu.make_async_remote_copy(
        src_ref=src,
        dst_ref=dst,
        send_sem=send,
        recv_sem=recv,
        device_id={"wide": to},
        device_id_type=MESH,
    )


def layer_kernel(
    lengths_hbm,
    occupied_hbm,
    queries,
    cache,
    w_uv,
    w_out,
    w_gate,
    w_up,
    w_down,
    residual_hbm,
    gain_hbm,
    out,
    lengths,
    occupied,
    residual,
    gain,
    gain_rows,
    scaled,
    q_v,
    c_v,
    uv_v,
    wo_v,
    gu_v,
    wd_v,
    load_sem,
    attn,
    a2a_out,
    a2a_in,
    a2a_send,
    a2a_recv,
    rowvals,
    values,
    acc,
    s0,
    rd,
    pair_of_send,
    pair_of_recv,
    rd_send,
    rd_recv,
    res_own,
    res_both,
    hid,
    sq_own,
    sq_in,
    gathered,
    ag_send,
    ag_recv,
    swap_send,
    swap_recv,
    up_own,
    acts,
    ends,
    last_own,
    last_in,
    pair_send,
    pair_recv,
):
    me = lax.axis_index("wide")
    core = lax.rem(me, 2)
    chip = me // 2
    x = lax.rem(chip, SIDE)
    y = chip // SIDE
    partner = me + 1 - 2 * core

    def at(cy, cx):
        return (cy * SIDE + cx) * 2 + core

    def along_x(k):
        return lax.rem(x + k, SIDE)

    def along_y(k):
        return lax.rem(y + k, SIDE)

    loads = []

    def load(src, dst, same=0):
        copy = pltpu.make_async_copy(src, dst, load_sem.at[len(loads) - same])
        copy.start()
        if not same:
            loads.append(copy)
        return copy

    count_loads = [load(lengths_hbm, lengths), load(occupied_hbm, occupied)]
    query_loads = []
    cache_loads = []
    for part in [pl.ds(s, 1) for s in range(WAVE)] + [pl.ds(WAVE, WAVE)]:
        query_loads.append(load(queries.at[part], q_v.at[part]))
        cache_loads.append(load(cache.at[part], c_v.at[part]))

    barrier = pltpu.get_barrier_semaphore()

    def greet(k, carry):
        pl.semaphore_signal(
            barrier, inc=1, device_id={"wide": lax.rem(me + k, DEVICES)}, device_id_type=MESH
        )
        return carry

    lax.fori_loop(1, DEVICES, greet, 0)
    row_loads = [load(residual_hbm, residual), load(gain_hbm, gain)]
    for h in range(OWN_HEADS):
        load(w_uv.at[h], uv_v.at[:, pl.ds(h * 128, 128)], same=min(h, 1))
    uv_sem = load_sem.at[len(loads) - 1]
    own_half = pl.ds(pl.multiple_of(core * HALF, 128), HALF)
    wo_loads = [load(w_out.at[:, own_half], wo_v.at[core])]
    load(w_gate, gu_v.at[pl.ds(0, FFS)])
    load(w_up, gu_v.at[pl.ds(FFS, FFS)], same=1)
    gu_sem = load_sem.at[len(loads) - 1]
    wd_loads = [load(w_down.at[:, own_half], wd_v.at[core])]

    def upper(rows):
        return lax.broadcasted_iota(jnp.int32, rows.shape, 0) < WAVE

    def stack(rows, more):
        return jnp.where(upper(rows), rows, pltpu.roll(more, WAVE, 0))

    def stack_last(rows, more):
        return jnp.where(upper(rows), pltpu.roll(rows, WAVE, 0), more)

    position = lax.broadcasted_iota(jnp.int32, (HEADS, LMAX), 1)

    def attend(w):
        for i in range(WAVE):
            s = w * WAVE + i
            if s <= WAVE:
                query_loads[s].wait()
                cache_loads[s].wait()
            keys = c_v[s]
            scores = lax.dot_general(q_v[s], keys, TN, preferred_element_type=F32)
            scores = jnp.where(position < lengths[s], scores, F32(-1e30))
            peak = jnp.max(scores, axis=1, keepdims=True)
            weights = jnp.exp((scores - peak) * F32(softmax_scale))
            flag = occupied[s].astype(F32)
            probs = (weights * (flag / jnp.sum(weights, axis=1, keepdims=True))).astype(BF16)
            result = lax.dot_general(probs, keys[:LAT], NT, preferred_element_type=F32)
            for lane in range(LANES):
                attn[lane, i] = result[:, lane * 128 : (lane + 1) * 128]

        def pack(t, carry):
            for lane in range(LANES):
                tile = [attn[lane, i, pl.ds(pl.multiple_of(8 * t, 8), 8)] for i in range(WAVE)]
                for odd, join in enumerate((stack, stack_last)):
                    rows = jnp.concatenate([join(tile[0], tile[1]), join(tile[2], tile[3])], axis=0)
                    a2a_out[w, 2 * t + odd, :, lane * 128 : (lane + 1) * 128] = rows.astype(BF16)
            return carry

        lax.fori_loop(0, DEVICES // 2, pack, 0)

    def exchange(w):
        for dy, dx, dc in OFFSETS:
            to = (along_y(dy) * SIDE + along_x(dx)) * 2 + lax.rem(core + dc, 2)
            remote(
                a2a_out.at[w, to], a2a_in.at[w, me], a2a_send.at[w], a2a_recv.at[w], to
            ).start()
        a2a_in[w, me] = a2a_out[w, me]

    def project(w):
        others = a2a_in.at[w, pl.ds(0, DEVICES - 1)]
        wait_bytes(others, a2a_recv.at[w])
        wait_bytes(others, a2a_send.at[w])
        product = jnp.dot(
            a2a_in[w].reshape(DEVICES * OWN_HEADS * WAVE, LAT),
            uv_v[...],
            preferred_element_type=F32,
        )
        for h in range(OWN_HEADS):
            rowvals[h] = product[:, h * 128 : (h + 1) * 128]
        for h in range(OWN_HEADS):
            values[w, core, :, h * 128 : (h + 1) * 128] = rowvals[
                h, pl.ds(h, ROWS, stride=OWN_HEADS), :
            ].astype(BF16)

    def sum_pair(n, w, given, product):
        m = 2 * n + w
        place = given.at[w, core]
        copy = remote(place, place, pair_of_send.at[m], pair_of_recv.at[m], partner)
        copy.start()
        acc[w] = product(core).reshape(SIDE, SIDE, 8, HALF)
        copy.wait()
        acc[w] += product(1 - core).reshape(SIDE, SIDE, 8, HALF)

    def sum_start(n, w):
        m = 2 * n + w
        for i, (dy, dx) in enumerate(CHIP_OFFSETS):
            to = (along_y(dy), along_x(dx))
            s0[(m, *to)] = acc[(w, *to)].astype(BF16)
            remote(s0.at[(m, *to)], rd.at[m, i], rd_send.at[m], rd_recv.at[m], at(*to)).start()

    def sum_end(n, w):
        m = 2 * n + w
        wait_bytes(rd.at[m], rd_recv.at[m])
        wait_bytes(rd.at[m], rd_send.at[m])
        total = acc[w, y, x]
        for i in range(CHIPS - 1):
            total += rd[m, i].astype(F32)
        return total

    def hide(w):
        if w == 0:
            res_copy.wait()
        join = stack if w == 0 else stack_last
        rows = join(res_both[0], res_both[1]) + sum_end(0, w)
        rows = rows.astype(BF16).astype(F32)
        hid[w] = rows
        square = jnp.sum(rows * rows, axis=1, keepdims=True)
        sq_own[w] = jnp.broadcast_to(square, (8, 128))
        copy = remote(
            sq_own.at[w], sq_in.at[w], pair_send.at[1 + w], pair_recv.at[1 + w], partner
        )
        copy.start()
        return copy

    def gather(w, copy):
        copy.wait()
        inverse = lax.rsqrt((sq_own[w, :, :1] + sq_in[w, :, :1]) * F32(1.0 / D) + F32(1e-6))
        gathered[w, core, y, x] = (hid[w] * inverse * scaled[...]).astype(BF16)
        place = gathered.at[w, core, y, x]
        for dy, dx in CHIP_OFFSETS:
            to = at(along_y(dy), along_x(dx))
            remote(place, place, ag_send.at[w], ag_recv.at[w, dy], to).start()

    def forward(w):
        for dy in (2, 1, 3, 0):
            row = gathered.at[w, core, along_y((SIDE - dy) % SIDE)]
            wait_bytes(row.at[pl.ds(0, SIDE if dy else SIDE - 1)], ag_recv.at[w, dy])
            remote(row, row, swap_send.at[w], swap_recv.at[w], partner).start()

    def wide(w, j):
        rows = gathered[w, j].astype(F32).reshape(ROWS, HALF).astype(BF16)
        return lax.dot_general(
            gu_v[:, pl.ds(pl.multiple_of(j * HALF, 128), HALF)],
            rows,
            NT,
            preferred_element_type=F32,
        )

    def expand_own(w):
        up_own[w] = wide(w, core)

    def expand(w):
        wait_bytes(gathered.at[w, 1 - core], swap_recv.at[w])
        wait_bytes(gathered.at[w, 1 - core], swap_send.at[w])
        up = up_own[w] + wide(w, 1 - core)
        gate = up[:FFS]
        acts[w, core] = (gate / (1.0 + jnp.exp(-gate)) * up[FFS:]).astype(BF16)

    def inward(w):
        return lambda j: lax.dot_general(acts[w, j], wd_v[j], TN, preferred_element_type=F32)

    def finish(w):
        ends[w] = hid[w] + sum_end(1, w)

    for copy in count_loads:
        copy.wait()
    attend(0)
    pl.semaphore_wait(barrier, DEVICES - 1)
    exchange(0)
    for copy in row_loads:
        copy.wait()
    for j in range(2):
        res_own[j] = residual[:, j * HALF : (j + 1) * HALF].astype(F32)
    res_copy = remote(
        res_own.at[1 - core], res_both.at[core], pair_send.at[0], pair_recv.at[0], partner
    )
    res_copy.start()
    other_half = pl.ds(pl.multiple_of((1 - core) * HALF, 128), HALF)
    wo_copy = remote(
        w_out.at[:, other_half], wo_v.at[core], pair_send.at[4], pair_recv.at[4], partner
    )
    wd_copy = remote(
        w_down.at[:, other_half], wd_v.at[core], pair_send.at[5], pair_recv.at[5], partner
    )
    wo_copy.start()
    wd_copy.start()
    res_both[core] = res_own[core]
    attend(1)
    exchange(1)
    gain_rows[...] = gain[...].astype(F32)
    for t in range(HALF // 128):
        row = gain_rows[pl.ds(core * (HALF // 128) + t, 1), :]
        scaled[:, t * 128 : (t + 1) * 128] = jnp.broadcast_to(row, (8, 128))
    wait_bytes(uv_v, uv_sem)
    wo_loads[0].wait()

    def outward(w):
        return lambda j: jnp.dot(values[w, j], wo_v[j], preferred_element_type=F32)

    project(0)
    wo_copy.wait()
    sum_pair(0, 0, values, outward(0))
    sum_start(0, 0)
    project(1)
    sum_pair(0, 1, values, outward(1))
    sum_start(0, 1)
    square0 = hide(0)
    gather(0, square0)
    wait_bytes(gu_v, gu_sem)
    wd_loads[0].wait()
    wd_copy.wait()
    square1 = hide(1)
    gather(1, square1)
    forward(0)
    expand_own(0)
    expand(0)
    sum_pair(1, 0, acts, inward(0))
    sum_start(1, 0)
    forward(1)
    expand_own(1)
    expand(1)
    sum_pair(1, 1, acts, inward(1))
    sum_start(1, 1)
    finish(0)
    finish(1)
    last_own[0] = stack(ends[0], ends[1])
    last_own[1] = stack_last(ends[0], ends[1])
    last = remote(last_own.at[1 - core], last_in, pair_send.at[3], pair_recv.at[3], partner)
    last.start()
    for w in range(2):
        wait_bytes(gathered.at[w, core, pl.ds(0, SIDE - 1)], ag_send.at[w])
        wait_bytes(gathered.at[w, core, 0, pl.ds(0, SIDE - 1)], ag_send.at[w])
    last.wait()
    out[:, pl.ds(pl.multiple_of(core * HALF, 128), HALF)] = last_own[core].astype(BF16)
    out[:, pl.ds(pl.multiple_of((1 - core) * HALF, 128), HALF)] = last_in[...].astype(BF16)


def shards(
    queries, latent_cache, lengths, occupied, residual, w_uv, w_out, norm_gain, w_gate, w_up, w_down
):
    hbm = pl.BlockSpec(memory_space=pl.ANY)
    vmem = pl.BlockSpec(memory_space=pltpu.VMEM)
    dma = pltpu.SemaphoreType.DMA
    return pl.pallas_call(
        layer_kernel,
        out_shape=jax.ShapeDtypeStruct((SLOT, D), BF16),
        in_specs=[hbm] * 11,
        out_specs=vmem,
        scratch_shapes=[
            pltpu.SMEM((SLOT,), jnp.int32),
            pltpu.SMEM((SLOT,), jnp.int32),
            pltpu.VMEM((SLOT, D), BF16),
            pltpu.VMEM((D // 128, 128), BF16),
            pltpu.VMEM((D // 128, 128), F32),
            pltpu.VMEM((8, HALF), F32),
            pltpu.VMEM((SLOT, KEY, HEADS), BF16),
            pltpu.VMEM((SLOT, KEY, LMAX), BF16),
            pltpu.VMEM((LAT, OWN_HEADS * 128), BF16),
            pltpu.VMEM((2, OWN_HEADS * 128, HALF), BF16),
            pltpu.VMEM((2 * FFS, D), BF16),
            pltpu.VMEM((2, FFS, HALF), BF16),
            dma((18,)),
            pltpu.VMEM((LANES, WAVE, HEADS, 128), F32),
            pltpu.VMEM((2, DEVICES, OWN_HEADS * WAVE, LAT), BF16),
            pltpu.VMEM((2, DEVICES, OWN_HEADS * WAVE, LAT), BF16),
            dma((2,)),
            dma((2,)),
            pltpu.VMEM((OWN_HEADS, ROWS * OWN_HEADS, 128), F32),
            pltpu.VMEM((2, 2, ROWS, OWN_HEADS * 128), BF16),
            pltpu.VMEM((2, SIDE, SIDE, 8, HALF), F32),
            pltpu.VMEM((4, SIDE, SIDE, 8, HALF), BF16),
            pltpu.VMEM((4, CHIPS - 1, 8, HALF), BF16),
            dma((4,)),
            dma((4,)),
            dma((4,)),
            dma((4,)),
            pltpu.VMEM((2, SLOT, HALF), F32),
            pltpu.VMEM((2, SLOT, HALF), F32),
            pltpu.VMEM((2, 8, HALF), F32),
            pltpu.VMEM((2, 8, 128), F32),
            pltpu.VMEM((2, 8, 128), F32),
            pltpu.VMEM((2, 2, SIDE, SIDE, 8, HALF), BF16),
            dma((2,)),
            dma((2, SIDE)),
            dma((2,)),
            dma((2,)),
            pltpu.VMEM((2, 2 * FFS, ROWS), F32),
            pltpu.VMEM((2, 2, FFS, ROWS), BF16),
            pltpu.VMEM((2, 8, HALF), F32),
            pltpu.VMEM((2, SLOT, HALF), F32),
            pltpu.VMEM((SLOT, HALF), F32),
            dma((6,)),
            dma((6,)),
        ],
        compiler_params=pltpu.CompilerParams(
            collective_id=0, has_side_effects=True, vmem_limit_bytes=60 * 2**20
        ),
        cost_estimate=pl.CostEstimate(
            flops=3_600_000_000, bytes_accessed=15_000_000, transcendentals=500_000
        ),
    )(
        lengths,
        occupied,
        jnp.swapaxes(queries, 1, 2),
        jnp.swapaxes(latent_cache, 1, 2),
        w_uv,
        w_out,
        w_gate.T,
        w_up.T,
        w_down,
        residual,
        norm_gain.reshape(D // 128, 128),
    )


def solution(mesh):
    in_specs = (
        P(("rep", "wide"), None, None),
        P(("rep", "wide"), None, None),
        P(("rep", "wide")),
        P(("rep", "wide")),
        P(("rep", "wide"), None),
        P("wide", None, None),
        P("wide", None),
        P(),
        P(None, "wide"),
        P(None, "wide"),
        P("wide", None),
    )
    out_specs = P(("rep", "wide"), None)
    return jax.shard_map(shards, mesh=mesh, in_specs=in_specs, out_specs=out_specs, check_vma=False)
```

```python
import jax
import jax.numpy as jnp
from jax import lax
from jax.experimental import pallas as pl
from jax.experimental.pallas import tpu as pltpu
from jax.sharding import PartitionSpec as P

MESH = pl.DeviceIdType.MESH
F32 = jnp.float32
BF16 = jnp.bfloat16
softmax_scale = 192.0 ** (-0.5)

SIDE = 4
CHIPS = SIDE * SIDE
DEVICES = 2 * CHIPS
SLOT = 8
WAVE = SLOT // 2
HEADS = 128
OWN_HEADS = HEADS // DEVICES
LAT = 512
LANES = LAT // 128
KEY = 576
LMAX = 384
D = 3584
HALF = D // 2
ROWS = DEVICES * WAVE
FFS = 288
NT = (((1,), (1,)), ((), ()))
TN = (((0,), (0,)), ((), ()))


def hops(offset):
    return sum(min(step, SIDE - step) for step in offset[:2])


CHIP_OFFSETS = sorted(
    [(dy, dx) for dy in range(SIDE) for dx in range(SIDE)][1:], key=lambda offset: -hops(offset)
)

OFFSETS = sorted(
    [(dy, dx, dc) for dy in range(SIDE) for dx in range(SIDE) for dc in range(2)][1:],
    key=lambda offset: -hops(offset),
)


def wait_bytes(ref, sem):
    pltpu.make_async_copy(ref, ref, sem).wait()


def remote(src, dst, send, recv, to):
    return pltpu.make_async_remote_copy(
        src_ref=src,
        dst_ref=dst,
        send_sem=send,
        recv_sem=recv,
        device_id={"wide": to},
        device_id_type=MESH,
    )


def layer_kernel(
    lengths_hbm,
    occupied_hbm,
    queries,
    cache,
    w_uv,
    w_out,
    w_gate,
    w_up,
    w_down,
    residual_hbm,
    gain_hbm,
    out,
    lengths,
    occupied,
    residual,
    gain,
    gain_rows,
    scaled,
    q_v,
    c_v,
    uv_v,
    wo_v,
    gu_v,
    wd_v,
    load_sem,
    attn,
    a2a_out,
    a2a_in,
    a2a_send,
    a2a_recv,
    rowvals,
    values,
    acc,
    s0,
    rd,
    pair_of_send,
    pair_of_recv,
    rd_send,
    rd_recv,
    res_own,
    res_both,
    hid,
    sq_own,
    sq_in,
    gathered,
    ag_send,
    ag_recv,
    swap_send,
    swap_recv,
    up_own,
    acts,
    ends,
    last_own,
    last_in,
    pair_send,
    pair_recv,
):
    me = lax.axis_index("wide")
    core = lax.rem(me, 2)
    chip = me // 2
    x = lax.rem(chip, SIDE)
    y = chip // SIDE
    partner = me + 1 - 2 * core

    def at(cy, cx):
        return (cy * SIDE + cx) * 2 + core

    def along_x(k):
        return lax.rem(x + k, SIDE)

    def along_y(k):
        return lax.rem(y + k, SIDE)

    loads = []

    def load(src, dst, same=0):
        copy = pltpu.make_async_copy(src, dst, load_sem.at[len(loads) - same])
        copy.start()
        if not same:
            loads.append(copy)
        return copy

    count_loads = [load(lengths_hbm, lengths), load(occupied_hbm, occupied)]
    query_loads = []
    cache_loads = []
    for part in [pl.ds(s, 1) for s in range(WAVE)] + [pl.ds(WAVE, WAVE)]:
        query_loads.append(load(queries.at[part], q_v.at[part]))
        cache_loads.append(load(cache.at[part], c_v.at[part]))

    barrier = pltpu.get_barrier_semaphore()

    def greet(k, carry):
        pl.semaphore_signal(
            barrier, inc=1, device_id={"wide": lax.rem(me + k, DEVICES)}, device_id_type=MESH
        )
        return carry

    lax.fori_loop(1, DEVICES, greet, 0)
    row_loads = [load(residual_hbm, residual), load(gain_hbm, gain)]
    for h in range(OWN_HEADS):
        load(w_uv.at[h], uv_v.at[:, pl.ds(h * 128, 128)], same=min(h, 1))
    uv_sem = load_sem.at[len(loads) - 1]
    own_half = pl.ds(pl.multiple_of(core * HALF, 128), HALF)
    wo_loads = [load(w_out.at[:, own_half], wo_v.at[core])]
    load(w_gate, gu_v.at[pl.ds(0, FFS)])
    load(w_up, gu_v.at[pl.ds(FFS, FFS)], same=1)
    gu_sem = load_sem.at[len(loads) - 1]
    wd_loads = [load(w_down.at[:, own_half], wd_v.at[core])]

    def upper(rows):
        return lax.broadcasted_iota(jnp.int32, rows.shape, 0) < WAVE

    def stack(rows, more):
        return jnp.where(upper(rows), rows, pltpu.roll(more, WAVE, 0))

    def stack_last(rows, more):
        return jnp.where(upper(rows), pltpu.roll(rows, WAVE, 0), more)

    position = lax.broadcasted_iota(jnp.int32, (HEADS, LMAX), 1)

    def attend(w):
        for i in range(WAVE):
            s = w * WAVE + i
            if s <= WAVE:
                query_loads[s].wait()
                cache_loads[s].wait()
            keys = c_v[s]
            scores = lax.dot_general(q_v[s], keys, TN, preferred_element_type=F32)
            scores = jnp.where(position < lengths[s], scores, F32(-1e30))
            peak = jnp.max(scores, axis=1, keepdims=True)
            weights = jnp.exp((scores - peak) * F32(softmax_scale))
            flag = occupied[s].astype(F32)
            probs = (weights * (flag / jnp.sum(weights, axis=1, keepdims=True))).astype(BF16)
            result = lax.dot_general(probs, keys[:LAT], NT, preferred_element_type=F32)
            for lane in range(LANES):
                attn[lane, i] = result[:, lane * 128 : (lane + 1) * 128]

        def pack(t, carry):
            for lane in range(LANES):
                tile = [attn[lane, i, pl.ds(pl.multiple_of(8 * t, 8), 8)] for i in range(WAVE)]
                for odd, join in enumerate((stack, stack_last)):
                    rows = jnp.concatenate([join(tile[0], tile[1]), join(tile[2], tile[3])], axis=0)
                    a2a_out[w, 2 * t + odd, :, lane * 128 : (lane + 1) * 128] = rows.astype(BF16)
            return carry

        lax.fori_loop(0, DEVICES // 2, pack, 0)

    def exchange(w):
        for dy, dx, dc in OFFSETS:
            to = (along_y(dy) * SIDE + along_x(dx)) * 2 + lax.rem(core + dc, 2)
            remote(
                a2a_out.at[w, to], a2a_in.at[w, me], a2a_send.at[w], a2a_recv.at[w], to
            ).start()
        a2a_in[w, me] = a2a_out[w, me]

    def project(w):
        others = a2a_in.at[w, pl.ds(0, DEVICES - 1)]
        wait_bytes(others, a2a_recv.at[w])
        product = jnp.dot(
            a2a_in[w].reshape(DEVICES * OWN_HEADS * WAVE, LAT),
            uv_v[...],
            preferred_element_type=F32,
        )
        for h in range(OWN_HEADS):
            rowvals[h] = product[:, h * 128 : (h + 1) * 128]
        for h in range(OWN_HEADS):
            values[w, core, :, h * 128 : (h + 1) * 128] = rowvals[
                h, pl.ds(h, ROWS, stride=OWN_HEADS), :
            ].astype(BF16)

    def sum_pair(n, w, given, product):
        m = 2 * n + w
        place = given.at[w, core]
        copy = remote(place, place, pair_of_send.at[m], pair_of_recv.at[m], partner)
        copy.start()
        acc[w] = product(core).reshape(SIDE, SIDE, 8, HALF)
        copy.wait()
        acc[w] += product(1 - core).reshape(SIDE, SIDE, 8, HALF)

    def sum_start(n, w):
        m = 2 * n + w
        for i, (dy, dx) in enumerate(CHIP_OFFSETS):
            to = (along_y(dy), along_x(dx))
            s0[(m, *to)] = acc[(w, *to)].astype(BF16)
            remote(s0.at[(m, *to)], rd.at[m, i], rd_send.at[m], rd_recv.at[m], at(*to)).start()

    def sum_end(n, w):
        m = 2 * n + w
        wait_bytes(rd.at[m], rd_recv.at[m])
        total = acc[w, y, x]
        for i in range(CHIPS - 1):
            total += rd[m, i].astype(F32)
        return total

    def hide(w):
        if w == 0:
            res_copy.wait()
        join = stack if w == 0 else stack_last
        rows = join(res_both[0], res_both[1]) + sum_end(0, w)
        rows = rows.astype(BF16).astype(F32)
        hid[w] = rows
        square = jnp.sum(rows * rows, axis=1, keepdims=True)
        sq_own[w] = jnp.broadcast_to(square, (8, 128))
        copy = remote(
            sq_own.at[w], sq_in.at[w], pair_send.at[1 + w], pair_recv.at[1 + w], partner
        )
        copy.start()
        return copy

    def gather(w, copy):
        copy.wait()
        inverse = lax.rsqrt((sq_own[w, :, :1] + sq_in[w, :, :1]) * F32(1.0 / D) + F32(1e-6))
        gathered[w, core, y, x] = (hid[w] * inverse * scaled[...]).astype(BF16)
        place = gathered.at[w, core, y, x]
        for dy, dx in CHIP_OFFSETS:
            to = at(along_y(dy), along_x(dx))
            remote(place, place, ag_send.at[w], ag_recv.at[w, dy], to).start()

    def forward(w):
        for dy in (2, 1, 3, 0):
            row = gathered.at[w, core, along_y((SIDE - dy) % SIDE)]
            wait_bytes(row.at[pl.ds(0, SIDE if dy else SIDE - 1)], ag_recv.at[w, dy])
            remote(row, row, swap_send.at[w], swap_recv.at[w], partner).start()

    def wide(w, j):
        rows = gathered[w, j].astype(F32).reshape(ROWS, HALF).astype(BF16)
        return lax.dot_general(
            gu_v[:, pl.ds(pl.multiple_of(j * HALF, 128), HALF)],
            rows,
            NT,
            preferred_element_type=F32,
        )

    def expand_own(w):
        up_own[w] = wide(w, core)

    def expand(w):
        wait_bytes(gathered.at[w, 1 - core], swap_recv.at[w])
        up = up_own[w] + wide(w, 1 - core)
        gate = up[:FFS]
        acts[w, core] = (gate / (1.0 + jnp.exp(-gate)) * up[FFS:]).astype(BF16)

    def inward(w):
        return lambda j: lax.dot_general(acts[w, j], wd_v[j], TN, preferred_element_type=F32)

    def finish(w):
        ends[w] = hid[w] + sum_end(1, w)

    for copy in count_loads:
        copy.wait()
    attend(0)
    pl.semaphore_wait(barrier, DEVICES - 1)
    exchange(0)
    for copy in row_loads:
        copy.wait()
    for j in range(2):
        res_own[j] = residual[:, j * HALF : (j + 1) * HALF].astype(F32)
    res_copy = remote(
        res_own.at[1 - core], res_both.at[core], pair_send.at[0], pair_recv.at[0], partner
    )
    res_copy.start()
    other_half = pl.ds(pl.multiple_of((1 - core) * HALF, 128), HALF)
    wo_copy = remote(
        w_out.at[:, other_half], wo_v.at[core], pair_send.at[4], pair_recv.at[4], partner
    )
    wd_copy = remote(
        w_down.at[:, other_half], wd_v.at[core], pair_send.at[5], pair_recv.at[5], partner
    )
    wo_copy.start()
    wd_copy.start()
    res_both[core] = res_own[core]
    attend(1)
    exchange(1)
    gain_rows[...] = gain[...].astype(F32)
    for t in range(HALF // 128):
        row = gain_rows[pl.ds(core * (HALF // 128) + t, 1), :]
        scaled[:, t * 128 : (t + 1) * 128] = jnp.broadcast_to(row, (8, 128))
    wait_bytes(uv_v, uv_sem)
    wo_loads[0].wait()

    def outward(w):
        return lambda j: jnp.dot(values[w, j], wo_v[j], preferred_element_type=F32)

    project(0)
    wo_copy.wait()
    sum_pair(0, 0, values, outward(0))
    sum_start(0, 0)
    project(1)
    sum_pair(0, 1, values, outward(1))
    sum_start(0, 1)
    square0 = hide(0)
    gather(0, square0)
    wait_bytes(gu_v, gu_sem)
    wd_loads[0].wait()
    wd_copy.wait()
    square1 = hide(1)
    gather(1, square1)
    forward(0)
    expand_own(0)
    expand(0)
    sum_pair(1, 0, acts, inward(0))
    sum_start(1, 0)
    forward(1)
    expand_own(1)
    expand(1)
    sum_pair(1, 1, acts, inward(1))
    sum_start(1, 1)
    finish(0)
    finish(1)
    last_own[0] = stack(ends[0], ends[1])
    last_own[1] = stack_last(ends[0], ends[1])
    last = remote(last_own.at[1 - core], last_in, pair_send.at[3], pair_recv.at[3], partner)
    last.start()
    for w in range(2):
        wait_bytes(a2a_in.at[w, pl.ds(0, DEVICES - 1)], a2a_send.at[w])
        wait_bytes(rd.at[w], rd_send.at[w])
        wait_bytes(rd.at[2 + w], rd_send.at[2 + w])
        wait_bytes(gathered.at[w, core], swap_send.at[w])
        wait_bytes(gathered.at[w, core, pl.ds(0, SIDE - 1)], ag_send.at[w])
        wait_bytes(gathered.at[w, core, 0, pl.ds(0, SIDE - 1)], ag_send.at[w])
    last.wait()
    out[:, pl.ds(pl.multiple_of(core * HALF, 128), HALF)] = last_own[core].astype(BF16)
    out[:, pl.ds(pl.multiple_of((1 - core) * HALF, 128), HALF)] = last_in[...].astype(BF16)


def shards(
    queries, latent_cache, lengths, occupied, residual, w_uv, w_out, norm_gain, w_gate, w_up, w_down
):
    hbm = pl.BlockSpec(memory_space=pl.ANY)
    vmem = pl.BlockSpec(memory_space=pltpu.VMEM)
    dma = pltpu.SemaphoreType.DMA
    return pl.pallas_call(
        layer_kernel,
        out_shape=jax.ShapeDtypeStruct((SLOT, D), BF16),
        in_specs=[hbm] * 11,
        out_specs=vmem,
        scratch_shapes=[
            pltpu.SMEM((SLOT,), jnp.int32),
            pltpu.SMEM((SLOT,), jnp.int32),
            pltpu.VMEM((SLOT, D), BF16),
            pltpu.VMEM((D // 128, 128), BF16),
            pltpu.VMEM((D // 128, 128), F32),
            pltpu.VMEM((8, HALF), F32),
            pltpu.VMEM((SLOT, KEY, HEADS), BF16),
            pltpu.VMEM((SLOT, KEY, LMAX), BF16),
            pltpu.VMEM((LAT, OWN_HEADS * 128), BF16),
            pltpu.VMEM((2, OWN_HEADS * 128, HALF), BF16),
            pltpu.VMEM((2 * FFS, D), BF16),
            pltpu.VMEM((2, FFS, HALF), BF16),
            dma((18,)),
            pltpu.VMEM((LANES, WAVE, HEADS, 128), F32),
            pltpu.VMEM((2, DEVICES, OWN_HEADS * WAVE, LAT), BF16),
            pltpu.VMEM((2, DEVICES, OWN_HEADS * WAVE, LAT), BF16),
            dma((2,)),
            dma((2,)),
            pltpu.VMEM((OWN_HEADS, ROWS * OWN_HEADS, 128), F32),
            pltpu.VMEM((2, 2, ROWS, OWN_HEADS * 128), BF16),
            pltpu.VMEM((2, SIDE, SIDE, 8, HALF), F32),
            pltpu.VMEM((4, SIDE, SIDE, 8, HALF), BF16),
            pltpu.VMEM((4, CHIPS - 1, 8, HALF), BF16),
            dma((4,)),
            dma((4,)),
            dma((4,)),
            dma((4,)),
            pltpu.VMEM((2, SLOT, HALF), F32),
            pltpu.VMEM((2, SLOT, HALF), F32),
            pltpu.VMEM((2, 8, HALF), F32),
            pltpu.VMEM((2, 8, 128), F32),
            pltpu.VMEM((2, 8, 128), F32),
            pltpu.VMEM((2, 2, SIDE, SIDE, 8, HALF), BF16),
            dma((2,)),
            dma((2, SIDE)),
            dma((2,)),
            dma((2,)),
            pltpu.VMEM((2, 2 * FFS, ROWS), F32),
            pltpu.VMEM((2, 2, FFS, ROWS), BF16),
            pltpu.VMEM((2, 8, HALF), F32),
            pltpu.VMEM((2, SLOT, HALF), F32),
            pltpu.VMEM((SLOT, HALF), F32),
            dma((6,)),
            dma((6,)),
        ],
        compiler_params=pltpu.CompilerParams(
            collective_id=0, has_side_effects=True, vmem_limit_bytes=60 * 2**20
        ),
        cost_estimate=pl.CostEstimate(
            flops=3_600_000_000, bytes_accessed=15_000_000, transcendentals=500_000
        ),
    )(
        lengths,
        occupied,
        jnp.swapaxes(queries, 1, 2),
        jnp.swapaxes(latent_cache, 1, 2),
        w_uv,
        w_out,
        w_gate.T,
        w_up.T,
        w_down,
        residual,
        norm_gain.reshape(D // 128, 128),
    )


def solution(mesh):
    in_specs = (
        P(("rep", "wide"), None, None),
        P(("rep", "wide"), None, None),
        P(("rep", "wide")),
        P(("rep", "wide")),
        P(("rep", "wide"), None),
        P("wide", None, None),
        P("wide", None),
        P(),
        P(None, "wide"),
        P(None, "wide"),
        P("wide", None),
    )
    out_specs = P(("rep", "wide"), None)
    return jax.shard_map(shards, mesh=mesh, in_specs=in_specs, out_specs=out_specs, check_vma=False)
```
